32 devices in a mesh: ep: 16 (over z, y, x), etp: 2 (over core).
Axes of the slice: x: 2, y: 2, z: 4, core: 2. Of those that a mesh axis runs over, the one named last changes fastest.
Arguments:
- tokens: bfloat16 [1024, 7168], P('ep', 'etp'), may hold values from -6 to 6
- cotangent: bfloat16 [1024, 7168], P('ep', 'etp'), may hold values from -6 to 6
- expert_ids: int32 [1024, 8], P('ep'), may hold values from 0 to 15, all different within a row; in each aligned block of 64 rows (0 to 63, 64 to 127, ...) at most 40 rows name the same one
- routing_gate_weight: bfloat16 [1024, 8], P('ep'), may hold values from 0.049804688 to 1
- gate_projection_weight: bfloat16 [16, 7168, 2048], P('ep', None, 'etp'), may hold values from -0.0625 to 0.0625
- up_weight: bfloat16 [16, 7168, 2048], P('ep', None, 'etp'), may hold values from -0.0625 to 0.0625
- down_weight: bfloat16 [16, 2048, 7168], P('ep', 'etp'), may hold values from -0.125 to 0.125
Outputs:
- input_grad: bfloat16 [1024, 7168], P('ep', 'etp')
- gate_grad: float32 [1024, 8], P('ep')
- w_gate_grad: bfloat16 [16, 7168, 2048], P('ep', None, 'etp')
- w_up_grad: bfloat16 [16, 7168, 2048], P('ep', None, 'etp')
- w_down_grad: bfloat16 [16, 2048, 7168], P('ep', 'etp')
The draws below stay inside these ranges and needn't reach their ends.
Inputs may be any that keep to these rules, and one draw needn't show every extreme that they name: `expert_ids`: each row names 8 different experts. Among the rows of one index of ep no expert is named more than 40 times, a bound that some block reaches.
All inputs are finite; a program needn't handle non-finite values.
Results may differ from the reference program's by a relative error of at most 0.019.
Values may be sent and summed in bfloat16 or wider, within the bound.
A program may use at most 192 MiB of HBM per device.

```python
import math
import jax
import jax.numpy as jnp
import numpy as np
from jax import lax

D = 7168
FF = 2048
TOP = 8
TOK_EP = 64
TOKENS = 1024
EXPERT_COUNT = 16
EXPERT_ROOM = 40
N_EP = 16
N_ETP = 2


def block_levels(own_key, shape, split, smallest, high):
    def one(position, parts):
        steps = jax.random.uniform(jax.random.fold_in(jax.random.fold_in(own_key, 6), position), (parts,), jnp.float32, smallest / len(split), high / len(split))
        return jnp.repeat(jnp.exp(steps), shape[position] // parts).reshape((-1,) + (1,) * (len(shape) - position - 1))

    loudness = one(*split[0])
    for cut in split[1:]:
        loudness = loudness * one(*cut)
    return loudness


def shared_out(stream_key, own, number, rows, count, top, reach, lean):
    order = jax.random.permutation(stream_key, count)
    crowded, usual = portions_of(count, rows * top, reach, lean, True), portions_of(count, rows * top, reach, lean, False)
    places = jnp.arange(count)

    def named(tallies, rotation):
        used = int((tallies > 0).sum())
        fixed = max(1, used // 4)
        moved = fixed + (places - fixed + rotation * (used - fixed)) % max(1, count - fixed)
        return jnp.zeros((count,), jnp.int32).at[order[jnp.where(places < fixed, places, moved)]].set(jnp.asarray(tallies, jnp.int32))

    tallies = jnp.where(number % 4 == 0, named(crowded, number // 4), named(usual, number - number // 4 - 1))
    mixed = jax.random.permutation(jax.random.fold_in(own, 3), count)
    donor, receiver = mixed[0:count // 2 * 2:2], mixed[1:count // 2 * 2:2]
    room = jnp.minimum(tallies[donor] - 1, reach - tallies[receiver]) // 2
    room = jnp.where((donor == order[0]) | (receiver == order[0]) | (tallies[receiver] == 0), 0, jnp.maximum(room, 0))
    moved = jax.random.randint(jax.random.fold_in(own, 4), (count // 2,), 0, 1 << 20) % (room + 1)
    tallies = tallies.at[donor].add(-moved).at[receiver].add(moved)
    labels = jnp.searchsorted(jnp.cumsum(tallies), jnp.arange(rows * top), side="right").astype(jnp.int32)
    table = labels.reshape(top, rows).T
    table = table[jax.random.permutation(jax.random.fold_in(own, 1), rows)]
    rotation = jax.random.randint(jax.random.fold_in(own, 2), (rows, 1), 0, top)
    return jnp.take_along_axis(table, (jnp.arange(top)[None, :] + rotation) % top, axis=1)


def portions_of(amount, total, reach, lean, full):
    weights = [(1 << 20) // math.isqrt(rank ** lean) + 1 for rank in range(1, amount + 1)]
    largest = reach if full else min(reach, max(-(-total // amount), total * weights[0] // sum(weights)))
    least = 1 if total - largest >= amount - 1 else 0
    counts, surplus = [largest] + [least] * (amount - 1), total - largest - least * (amount - 1)
    while surplus > 0:
        free = [i for i in range(1, amount) if counts[i] < largest] or [i for i in range(1, amount) if counts[i] < reach]
        pool, budget = sum([weights[i] for i in free]), surplus
        for i in free:
            more = min(reach - counts[i], max(1, budget * weights[i] // pool), surplus)
            counts[i] = counts[i] + more
            surplus = surplus - more
    return np.array(counts)


def normal_values(rng, dims, scale, bound, pieces=(), kind=jnp.bfloat16):
    entries = scale * jax.random.normal(rng, dims, jnp.float32)
    if pieces:
        entries = entries * block_levels(rng, dims, pieces, -0.22, 0.18)
    return jnp.clip(entries, -bound, bound).astype(kind)


def setup_inputs(seed: int = 0) -> dict:
    arg_keys = jax.random.split(jax.random.key(seed), 8)
    tokens = normal_values(arg_keys[0], (TOKENS, D), 1.0, 6.0, ((0, 16), (1, 2)))
    cotangent = normal_values(arg_keys[1], (TOKENS, D), 1.0, 6.0, ((0, 16), (1, 2)))
    expert_ids_keys = jax.random.split(jax.random.fold_in(arg_keys[2], 1), TOKENS // TOK_EP)
    expert_ids_turns = jax.random.permutation(jax.random.fold_in(arg_keys[2], 3), TOKENS // TOK_EP)
    expert_ids = jax.vmap(lambda own, number: shared_out(jax.random.fold_in(arg_keys[2], 2), own, number, TOK_EP, EXPERT_COUNT, TOP, EXPERT_ROOM, 1))(expert_ids_keys, expert_ids_turns).reshape((TOKENS, TOP))
    routing_gate_weight = jnp.clip(jnp.exp(math.log(1.0) - 2.9996462 * jax.random.uniform(arg_keys[3], (TOKENS, TOP), jnp.float32) ** block_levels(arg_keys[3], (TOKENS, TOP), ((0, 16),), -0.2, 0.2)), 0.049804688, 1.0).astype(jnp.bfloat16)
    gate_projection_weight = normal_values(arg_keys[4], (EXPERT_COUNT, D, FF), D ** -0.5, 0.0625, ((0, 16), (2, 2)))
    up_weight = normal_values(arg_keys[5], (EXPERT_COUNT, D, FF), D ** -0.5, 0.0625, ((0, 16), (2, 2)))
    down_weight = normal_values(arg_keys[6], (EXPERT_COUNT, FF, D), FF ** -0.5, 0.125, ((0, 16), (1, 2)))
    return dict(tokens=tokens, cotangent=cotangent, expert_ids=expert_ids, routing_gate_weight=routing_gate_weight, gate_projection_weight=gate_projection_weight, up_weight=up_weight, down_weight=down_weight)


def pair_ranks(expert_ids):
    blocks = expert_ids.reshape(N_EP, TOK_EP * TOP)
    onehot = (blocks[:, :, None] == jnp.arange(EXPERT_COUNT, dtype=jnp.int32)[None, None, :]).astype(jnp.int32)
    before = jnp.cumsum(onehot, axis=1) - onehot
    return jnp.sum(before * onehot, axis=2).reshape(TOKENS, TOP).astype(jnp.int32)


def expert_gradient_pass(packed):
    xe, dye, ge, wg, wu, wd = packed
    a = jnp.dot(xe, wg, preferred_element_type=jnp.float32)
    b = jnp.dot(xe, wu, preferred_element_type=jnp.float32)
    sig = jax.nn.sigmoid(a)
    s = a * sig
    h = s * b
    gf = ge.astype(jnp.float32)[:, None]
    hs = (gf * h).astype(jnp.bfloat16)
    down_weight_gradient = jnp.dot(hs.T, dye, preferred_element_type=jnp.float32).astype(jnp.bfloat16)
    raw = jnp.dot(dye, wd.T, preferred_element_type=jnp.float32)
    slotted_gate = jnp.sum(h * raw, axis=1)
    dh = gf * raw
    da = (dh * b * sig * (1.0 + a * (1.0 - sig))).astype(jnp.bfloat16)
    db = (dh * s).astype(jnp.bfloat16)
    gate_weight_gradient = jnp.dot(xe.T, da, preferred_element_type=jnp.float32).astype(jnp.bfloat16)
    up_weight_gradient = jnp.dot(xe.T, db, preferred_element_type=jnp.float32).astype(jnp.bfloat16)
    width = FF // N_ETP
    total = jnp.zeros((xe.shape[0], D), jnp.float32)
    for group in range(N_ETP):
        lo = group * width
        part = jnp.dot(da[:, lo:lo + width], wg[:, lo:lo + width].T, preferred_element_type=jnp.float32)
        part = part + jnp.dot(db[:, lo:lo + width], wu[:, lo:lo + width].T, preferred_element_type=jnp.float32)
        total = total + lax.optimization_barrier(part.astype(jnp.bfloat16)).astype(jnp.float32)
    return gate_weight_gradient, up_weight_gradient, down_weight_gradient, total, slotted_gate


def reference(tokens, cotangent, expert_ids, routing_gate_weight, gate_projection_weight, up_weight, down_weight):
    rank = pair_ranks(expert_ids)
    block = (jnp.arange(TOKENS, dtype=jnp.int32) // TOK_EP).astype(jnp.int32)
    target_slot = (expert_ids * (N_EP * EXPERT_ROOM) + block[:, None] * EXPERT_ROOM + rank).reshape(-1).astype(jnp.int32)
    source = jnp.repeat(jnp.arange(TOKENS, dtype=jnp.int32), TOP)
    slot_positions = EXPERT_COUNT * N_EP * EXPERT_ROOM
    input_buffer = jnp.zeros((slot_positions, D), jnp.bfloat16).at[target_slot].set(tokens[source]).reshape(EXPERT_COUNT, N_EP * EXPERT_ROOM, D)
    output_gradient_buffer = jnp.zeros((slot_positions, D), jnp.bfloat16).at[target_slot].set(cotangent[source]).reshape(EXPERT_COUNT, N_EP * EXPERT_ROOM, D)
    gate_buffer = jnp.zeros((slot_positions,), jnp.bfloat16).at[target_slot].set(routing_gate_weight.reshape(-1)).reshape(EXPERT_COUNT, N_EP * EXPERT_ROOM)
    gate_weight_gradient, up_weight_gradient, down_weight_gradient, slotted_input, slotted_gate = lax.map(expert_gradient_pass, (input_buffer, output_gradient_buffer, gate_buffer, gate_projection_weight, up_weight, down_weight))
    picked = slotted_input.reshape(slot_positions, D)[target_slot].reshape(TOKENS, TOP, D)
    input_grad = jnp.sum(picked, axis=1).astype(jnp.bfloat16)
    gate_grad = slotted_gate.reshape(slot_positions)[target_slot].reshape(TOKENS, TOP)
    return input_grad, gate_grad, gate_weight_gradient, up_weight_gradient, down_weight_gradient
```

```python
import math

import jax
import jax.numpy as jnp
from jax import lax
from jax.sharding import PartitionSpec as P

F32 = jnp.float32
BF16 = jnp.bfloat16


def local(
    tokens,
    cotangent,
    expert_ids,
    routing_gate_weight,
    gate_projection_weight,
    up_weight,
    down_weight,
):
    ep_count = lax.axis_size("ep")
    me = lax.axis_index("ep")
    rows, cols = tokens.shape
    choose = expert_ids.shape[1]
    capacity = min(rows, rows * choose * 5 // (4 * ep_count))
    total_rows = ep_count * rows
    slots = ep_count * capacity
    per = math.gcd(max(1, 256 // rows), ep_count)
    groups = ep_count // per

    routes = jnp.concatenate(
        [expert_ids.astype(F32), routing_gate_weight.astype(F32)], axis=1
    )
    routes = lax.all_gather(routes, "ep", axis=0, tiled=True)
    x_all = lax.all_gather(tokens, "ep", axis=0, tiled=True)
    x_all, cotangent = lax.optimization_barrier((x_all, cotangent))
    dy_all = lax.all_gather(cotangent, "ep", axis=0, tiled=True)

    hit = routes[:, :choose] == me.astype(F32)
    gate = jnp.sum(jnp.where(hit, routes[:, choose:], 0.0), axis=1)
    named = jnp.any(hit, axis=1).reshape(ep_count, rows)
    rank = jnp.cumsum(named.astype(jnp.int32), axis=1) - 1
    place = rank + (jnp.arange(ep_count, dtype=jnp.int32) % per)[:, None] * capacity
    place = jnp.where(named, place, -1).reshape(groups, 1, per * rows)
    pick = place == jnp.arange(per * capacity, dtype=jnp.int32)[None, :, None]
    select = pick.astype(BF16)
    gf = jnp.sum(jnp.where(pick, gate.reshape(groups, 1, per * rows), 0.0), axis=2)
    gf = gf.reshape(slots, 1)

    def dispatch(all_rows):
        out = jnp.einsum(
            "gst,gtc->gsc",
            select,
            all_rows.reshape(groups, per * rows, cols),
            preferred_element_type=F32,
        )
        out = out.astype(BF16).reshape(slots, cols)
        return lax.all_gather(out, "etp", axis=1, tiled=True)

    wg = gate_projection_weight[0]
    wu = up_weight[0]
    wd = down_weight[0]
    xe = dispatch(x_all)
    a = jnp.dot(xe, wg, preferred_element_type=F32)
    b = jnp.dot(xe, wu, preferred_element_type=F32)
    dye = dispatch(dy_all)
    raw = jnp.dot(dye, wd.T, preferred_element_type=F32)
    sig = jax.nn.sigmoid(a)
    s = a * sig
    h = s * b
    hs = (gf * h).astype(BF16)
    gate_local = jnp.sum(h * raw, axis=1)
    dh = gf * raw
    da = (dh * b * sig * (1.0 + a * (1.0 - sig))).astype(BF16)
    db = (dh * s).astype(BF16)
    partial_value = jnp.dot(da, wg.T, preferred_element_type=F32) + jnp.dot(
        db, wu.T, preferred_element_type=F32
    )
    share = lax.psum_scatter(
        partial_value.astype(BF16), "etp", scatter_dimension=1, tiled=True
    )
    dense = jnp.einsum(
        "gst,gsc->gtc",
        select,
        share.reshape(groups, per * capacity, cols),
        preferred_element_type=F32,
    )
    dense = dense.astype(BF16).reshape(total_rows, cols)
    input_grad = lax.psum_scatter(dense, "ep", scatter_dimension=0, tiled=True)

    gate_rows = jnp.sum(
        jnp.where(pick, gate_local.reshape(groups, per * capacity, 1), 0.0), axis=1
    )
    gate_rows = lax.psum(gate_rows.reshape(ep_count, rows), "etp")
    gate_back = lax.all_to_all(gate_rows, "ep", split_axis=0, concat_axis=0, tiled=True)
    wanted = expert_ids[:, :, None] == jnp.arange(ep_count, dtype=jnp.int32)[None, None, :]
    gate_grad = jnp.sum(jnp.where(wanted, gate_back.T[:, None, :], 0.0), axis=2)

    down_weight_gradient = jnp.dot(hs.T, dye, preferred_element_type=F32).astype(BF16)
    gate_weight_gradient = jnp.dot(xe.T, da, preferred_element_type=F32).astype(BF16)
    up_weight_gradient = jnp.dot(xe.T, db, preferred_element_type=F32).astype(BF16)
    return (
        input_grad,
        gate_grad,
        gate_weight_gradient[None],
        up_weight_gradient[None],
        down_weight_gradient[None],
    )


def solution(mesh):
    in_specs = (
        P("ep", "etp"),
        P("ep", "etp"),
        P("ep", None),
        P("ep", None),
        P("ep", None, "etp"),
        P("ep", None, "etp"),
        P("ep", "etp", None),
    )
    out_specs = (
        P("ep", "etp"),
        P("ep", None),
        P("ep", None, "etp"),
        P("ep", None, "etp"),
        P("ep", "etp", None),
    )
    return jax.shard_map(local, mesh=mesh, in_specs=in_specs, out_specs=out_specs, check_vma=False)
```

```python
import math

import jax
import jax.numpy as jnp
from jax import lax
from jax.sharding import PartitionSpec as P

F32 = jnp.float32
BF16 = jnp.bfloat16


OFFSETS = (0, 1, -1, 2)


def shift(value, offset):
    n = lax.axis_size("ep")
    return lax.ppermute(value, "ep", [(i, (i + 4 * offset) % n) for i in range(n)])


def swap(value, bits):
    n = lax.axis_size("ep")
    return lax.ppermute(value, "ep", [(i, i ^ bits) for i in range(n)])


def swap_core(value):
    return lax.ppermute(value, "etp", [(0, 1), (1, 0)])


def spread_plane(value):
    half = value.shape[1] // 2
    by_x = swap(value, 1)
    by_y = swap(value, 2)
    lower = swap(by_y[:, :half], 1)
    upper = swap(by_x[:, half:], 2)
    return by_x, by_y, lower, upper


def gather_planes(block, after=None):
    if after is not None:
        block = lax.optimization_barrier((block,) + tuple(after))[0]
    far = [shift(block, -offset) for offset in OFFSETS[1:]]
    near = jnp.stack(far[:2])
    planes = []
    for batch in (block[None], near, far[2][None]):
        by_x, by_y, lower, upper = spread_plane(batch)
        for k in range(batch.shape[0]):
            planes.append(
                jnp.concatenate([batch[k], by_x[k], by_y[k], lower[k], upper[k]], axis=0)
            )
    return planes, far


def reduce_planes(dense):
    half = dense.shape[2] // 2
    from_x = swap(dense[:, 3, :half], 1)
    from_y = swap(dense[:, 3, half:], 2)
    for_y = jnp.concatenate(
        [
            (dense[:, 2, :half].astype(F32) + from_x.astype(F32)).astype(BF16),
            dense[:, 2, half:],
        ],
        axis=1,
    )
    for_x = jnp.concatenate(
        [
            dense[:, 1, :half],
            (dense[:, 1, half:].astype(F32) + from_y.astype(F32)).astype(BF16),
        ],
        axis=1,
    )
    got_y = swap(for_y, 2)
    got_x = swap(for_x, 1)
    total = (dense[:, 0].astype(F32) + got_x.astype(F32) + got_y.astype(F32)).astype(BF16)
    result = total[0].astype(F32)
    for k in range(1, 4):
        result = result + shift(total[k], OFFSETS[k]).astype(F32)
    return result.astype(BF16)


def local(
    tokens,
    cotangent,
    expert_ids,
    routing_gate_weight,
    gate_projection_weight,
    up_weight,
    down_weight,
):
    ep_count = lax.axis_size("ep")
    me = lax.axis_index("ep")
    core = lax.axis_index("etp")
    rows, cols = tokens.shape
    choose = expert_ids.shape[1]
    capacity = min(rows, rows * choose * 5 // (4 * ep_count))
    slots = ep_count * capacity
    pair = lax.axis_size("etp") == 2
    stepwise = ep_count == 16 and pair
    per = 4 if stepwise else math.gcd(max(1, 256 // rows), ep_count)
    groups = ep_count // per

    pad = -2 * choose % 128
    block = jnp.concatenate(
        [
            tokens,
            expert_ids.astype(BF16),
            routing_gate_weight,
            jnp.zeros((rows, pad), BF16),
        ],
        axis=1,
    )
    if stepwise:
        x_groups, far = gather_planes(block)
        dy_groups, _ = gather_planes(cotangent, far)
        offsets = jnp.asarray(OFFSETS, jnp.int32)[:, None]
        places = jnp.arange(4, dtype=jnp.int32)[None, :]
        blocks = ((me // 4 + offsets) % 4 * 4 + (me % 4 ^ places)).reshape(-1)
    else:
        x_all = lax.all_gather(block, "ep", axis=0, tiled=True)
        dy_all = lax.all_gather(cotangent, "ep", axis=0, tiled=True)
        x_groups = list(x_all.reshape(groups, per * rows, -1))
        dy_groups = list(dy_all.reshape(groups, per * rows, -1))
        blocks = jnp.arange(ep_count, dtype=jnp.int32)

    routes = jnp.concatenate([g[:, cols : cols + 2 * choose] for g in x_groups], axis=0)
    routes = routes.astype(F32)
    hit = routes[:, :choose] == me.astype(F32)
    gate = jnp.sum(jnp.where(hit, routes[:, choose:], 0.0), axis=1)
    named = jnp.any(hit, axis=1).reshape(ep_count, rows)
    rank = jnp.cumsum(named.astype(jnp.int32), axis=1) - 1
    place = rank + (jnp.arange(ep_count, dtype=jnp.int32) % per)[:, None] * capacity
    place = jnp.where(named, place, -1).reshape(groups, 1, per * rows)
    pick = place == jnp.arange(per * capacity, dtype=jnp.int32)[None, :, None]
    select = pick.astype(BF16)
    gf = jnp.sum(jnp.where(pick, gate.reshape(groups, 1, per * rows), 0.0), axis=2)
    gf = gf.reshape(slots, 1)

    def dispatch(parts):
        return jnp.concatenate(
            [
                jnp.dot(select[i], part[:, :cols], preferred_element_type=F32).astype(BF16)
                for i, part in enumerate(parts)
            ],
            axis=0,
        )

    wg = gate_projection_weight[0]
    wu = up_weight[0]
    wd = down_weight[0]
    xe = lax.all_gather(dispatch(x_groups), "etp", axis=1, tiled=True)
    a = jnp.dot(xe, wg, preferred_element_type=F32)
    b = jnp.dot(xe, wu, preferred_element_type=F32)
    dy_own = dispatch(dy_groups)
    own_start, other_start = core * cols, (1 - core) * cols
    if pair:
        dy_other = swap_core(dy_own)
        dy_own, a, b = lax.optimization_barrier((dy_own, a, b))
        raw = jnp.dot(
            dy_own, lax.dynamic_slice_in_dim(wd, own_start, cols, 1).T, preferred_element_type=F32
        ) + jnp.dot(
            dy_other,
            lax.dynamic_slice_in_dim(wd, other_start, cols, 1).T,
            preferred_element_type=F32,
        )
    else:
        dye = lax.all_gather(dy_own, "etp", axis=1, tiled=True)
        raw = jnp.dot(dye, wd.T, preferred_element_type=F32)
    sig = jax.nn.sigmoid(a)
    s = a * sig
    h = s * b
    hs = (gf * h).astype(BF16)
    gate_local = jnp.sum(h * raw, axis=1)
    dh = gf * raw
    da = (dh * b * sig * (1.0 + a * (1.0 - sig))).astype(BF16)
    db = (dh * s).astype(BF16)

    def part(start, width):
        return (
            jnp.dot(
                da, lax.dynamic_slice_in_dim(wg, start, width, 0).T, preferred_element_type=F32
            )
            + jnp.dot(
                db, lax.dynamic_slice_in_dim(wu, start, width, 0).T, preferred_element_type=F32
            )
        ).astype(BF16)

    pieces = 2 if pair else 1
    width = cols // pieces
    grads = []
    last = None
    for i in range(pieces):
        if pair:
            theirs = part(other_start + i * width, width)
            arrived = swap_core(theirs)
            mine = part(own_start + i * width, width)
            last = mine
            share = (mine.astype(F32) + arrived.astype(F32)).astype(BF16)
        else:
            last = part(0, wg.shape[0])
            share = lax.psum_scatter(last, "etp", scatter_dimension=1, tiled=True)
        dense = jnp.einsum(
            "gst,gsc->gtc",
            select,
            share.reshape(groups, per * capacity, width),
            preferred_element_type=F32,
        ).astype(BF16)
        if stepwise:
            grads.append(reduce_planes(dense.reshape(4, 4, rows, width)))
        else:
            grads.append(
                lax.psum_scatter(
                    dense.reshape(ep_count * rows, width), "ep", scatter_dimension=0, tiled=True
                )
            )
    input_grad = jnp.concatenate(grads, axis=1)

    gate_rows = jnp.sum(
        jnp.where(pick, gate_local.reshape(groups, per * capacity, 1), 0.0), axis=1
    ).reshape(ep_count, 1, rows)
    order = blocks[:, None] == jnp.arange(ep_count, dtype=jnp.int32)[None, :]
    gate_rows = jnp.sum(jnp.where(order[:, :, None], gate_rows, 0.0), axis=0)
    gate_rows = lax.psum(gate_rows, "etp")
    gate_back = lax.all_to_all(gate_rows, "ep", split_axis=0, concat_axis=0, tiled=True)
    wanted = expert_ids[:, :, None] == jnp.arange(ep_count, dtype=jnp.int32)[None, None, :]
    gate_grad = jnp.sum(jnp.where(wanted, gate_back.T[:, None, :], 0.0), axis=2)

    hs, da_late, db_late, _ = lax.optimization_barrier((hs, da, db, last))
    if pair:
        first = core == 0
        dye = jnp.concatenate(
            [jnp.where(first, dy_own, dy_other), jnp.where(first, dy_other, dy_own)], axis=1
        )
    gate_weight_gradient = jnp.dot(xe.T, da_late, preferred_element_type=F32).astype(BF16)
    up_weight_gradient = jnp.dot(xe.T, db_late, preferred_element_type=F32).astype(BF16)
    down_weight_gradient = jnp.dot(hs.T, dye, preferred_element_type=F32).astype(BF16)
    return (
        input_grad,
        gate_grad,
        gate_weight_gradient[None],
        up_weight_gradient[None],
        down_weight_gradient[None],
    )


def solution(mesh):
    in_specs = (
        P("ep", "etp"),
        P("ep", "etp"),
        P("ep", None),
        P("ep", None),
        P("ep", None, "etp"),
        P("ep", None, "etp"),
        P("ep", "etp", None),
    )
    out_specs = (
        P("ep", "etp"),
        P("ep", None),
        P("ep", None, "etp"),
        P("ep", None, "etp"),
        P("ep", "etp", None),
    )
    return jax.shard_map(local, mesh=mesh, in_specs=in_specs, out_specs=out_specs, check_vma=False)
```
